256 devices in a mesh: ep: 16 (over x_lo, z), fsdp: 8 (over y, x_hi), rep: 2 (over core).
Axes of the slice: x: 4 (x_hi: 2, x_lo: 2; x = x_hi * 2 + x_lo), y: 4, z: 8, core: 2. Of those that a mesh axis runs over, the one named last changes fastest.
Arguments:
- weights: bfloat16 [32, 2048, 7168], P(('ep', 'rep'), None, 'fsdp'), may hold values from -6 to 6
- owner_map: int32 [32], replicated, may hold values from 0 to 63
Outputs:
- quant: bfloat16 [32, 8, 256, 7168], P(None, 'fsdp', ('ep', 'rep'))
- block_scales: float32 [32, 16, 56], P(None, 'fsdp')
The draws below stay inside these ranges and needn't reach their ends.
All inputs are finite; a program needn't handle non-finite values. Where the reference program divides by a largest or mean magnitude, that divisor is 1e-20 or more.
Results may differ from the reference program's by a relative error of at most 0.0057.
Values may be sent and summed in bfloat16 or wider, within the bound.
A program may use at most 64 MiB of HBM per device.

```python
import math
import jax
import jax.numpy as jnp
from jax import lax

D = 7168
HID = 2048
HAD = 128
QB = 128
COS = 56
EXPERTS = 32
OWNERS = 64
N_FSDP = 8


def set_ends(values, own_key, low, top_value):
    longest = values.shape.index(max(values.shape))
    spots = []
    for shift in (0, 1):
        where = [jax.random.randint(jax.random.fold_in(own_key, axis), (), 0, length) for axis, length in enumerate(values.shape)]
        where[longest] = (where[longest] + shift) % values.shape[longest]
        spots.append(tuple(where))
    return values.at[spots[0]].set(low).at[spots[1]].set(top_value)


def levels(rng, dims, split, least, high):
    factor_of = 1.0
    for dim, shards_of in split:
        steps = jax.random.uniform(jax.random.fold_in(jax.random.fold_in(rng, 6), dim), (shards_of,), jnp.float32, least / len(split), high / len(split))
        factor_of = factor_of * jnp.repeat(jnp.exp(steps), dims[dim] // shards_of).reshape((-1,) + (1,) * (len(dims) - 1 - dim))
    return factor_of


def normal_values(stream_key, extent, spread, bound, split=(), kind=jnp.bfloat16):
    gain = levels(stream_key, extent, split, -0.22, 0.18) if split else 1.0
    drawn = jax.random.normal(stream_key, extent, jnp.float32) * spread * gain
    return jnp.minimum(jnp.maximum(drawn, -bound), bound).astype(kind)


def setup_inputs(seed: int = 0) -> dict:
    keys = jax.random.split(jax.random.key(seed), 3)
    return {
        "weights": normal_values(keys[0], (EXPERTS, HID, D), 1.0, 6.0, ((0, 32), (2, 8))),
        "owner_map": set_ends(jax.random.randint(keys[1], (EXPERTS,), 0, OWNERS), jax.random.fold_in(keys[1], 1), 0, OWNERS - 1).astype(jnp.int32),
    }


epsilon = 1e-06

def tables():
    lane_ids = jnp.arange(HAD, dtype=jnp.int32)
    anded = jnp.bitwise_and(lane_ids[:, None], lane_ids[None, :])
    parity = jnp.zeros((HAD, HAD), jnp.int32)
    for bit_pos in range(HAD.bit_length() - 1):
        parity = parity + jnp.bitwise_and(jnp.right_shift(anded, bit_pos), 1)
    signs_table = (1 - 2 * (parity % 2)).astype(jnp.float32).astype(jnp.bfloat16)
    freq_ids = jnp.arange(COS, dtype=jnp.float32)[:, None]
    cell_ids = jnp.arange(COS, dtype=jnp.float32)[None, :]
    cosine = jnp.sqrt(jnp.float32(2.0 / COS)) * jnp.cos(jnp.float32(math.pi) * (2.0 * cell_ids + 1.0) * freq_ids / (2.0 * COS))
    cosine = jnp.where(freq_ids == 0.0, cosine * jnp.float32(math.sqrt(0.5)), cosine)
    return (signs_table, cosine.astype(jnp.bfloat16))

def positions(owner_map):
    count = owner_map.shape[0]
    expert_ids = jnp.arange(count, dtype=jnp.int32)
    before = (owner_map[None, :] < owner_map[:, None]) | (owner_map[None, :] == owner_map[:, None]) & (expert_ids[None, :] < expert_ids[:, None])
    place = lax.optimization_barrier(jnp.sum(before.astype(jnp.int32), axis=1)).astype(jnp.int32)
    chosen = jnp.where(place[None, :] == expert_ids[:, None], expert_ids[None, :], 0)
    return lax.optimization_barrier(jnp.sum(chosen, axis=1)).astype(jnp.int32)

def reference(weights, owner_map):
    signs_table, cos_table = tables()
    inv_root = jnp.float32(1.0 / math.sqrt(HAD))

    def convert(single):
        parts = single.reshape(HID, COS, HAD).astype(jnp.float32)
        half_turned = (jnp.einsum('rji,ih->rjh', parts, signs_table.astype(jnp.float32), precision=lax.Precision.HIGHEST) * inv_root).astype(jnp.bfloat16)
        rotated = jnp.einsum('kj,rjh->rkh', cos_table.astype(jnp.float32), half_turned.astype(jnp.float32), precision=lax.Precision.HIGHEST)
        blocked = rotated.reshape(HID // QB, QB, COS, HAD)
        block_scale = lax.optimization_barrier(jnp.max(jnp.abs(blocked), axis=(1, 3))) + jnp.float32(epsilon)
        scaled = (blocked / block_scale[:, None, :, None]).astype(jnp.bfloat16).reshape(HID, D)
        return (scaled, block_scale)
    scaled, block_scale = lax.map(convert, weights)
    new_order = positions(owner_map)
    quant = jnp.take(scaled, new_order, axis=0).reshape(EXPERTS, N_FSDP, HID // N_FSDP, D)
    block_scales = jnp.take(block_scale, new_order, axis=0)
    return (quant, block_scales)
```

```python
import math

import jax
import jax.numpy as jnp
import ml_dtypes
import numpy as np
from jax import lax
from jax.experimental import pallas as pl
from jax.experimental.pallas import tpu as pltpu
from jax.sharding import PartitionSpec as P

MESH = pl.DeviceIdType.MESH
D = 7168
HAD = 128
COS = 56
WIDE = 896
TILES = WIDE // HAD
ROWS = 16
WAVES = 8
GROUP = 16
EPS = 1e-06


def hadamard():
    i = np.arange(HAD)
    both = i[:, None] & i[None, :]
    ones = sum((both >> bit) & 1 for bit in range(7))
    return (1 - 2 * (ones % 2)).astype(np.float32)


def cosine():
    k = np.arange(COS, dtype=np.float64)[:, None]
    j = np.arange(COS, dtype=np.float64)[None, :]
    c = np.sqrt(2.0 / COS) * np.cos(np.pi * (2 * j + 1) * k / (2 * COS))
    c[0] *= np.sqrt(0.5)
    return c.astype(ml_dtypes.bfloat16).astype(np.float32)


def positions(owner_map):
    count = owner_map.shape[0]
    ids = jnp.arange(count, dtype=jnp.int32)
    before = (owner_map[None, :] < owner_map[:, None]) | (
        (owner_map[None, :] == owner_map[:, None]) & (ids[None, :] < ids[:, None])
    )
    place = jnp.sum(before.astype(jnp.int32), axis=1)
    chosen = jnp.where(place[None, :] == ids[:, None], ids[None, :], 0)
    return jnp.sum(chosen, axis=1)


def device(z, x, y, c):
    return (lax.rem(x, 2) * 8 + z, y * 2 + x // 2, c)


def place():
    ep, fsdp, core = lax.axis_index("ep"), lax.axis_index("fsdp"), lax.axis_index("rep")
    return lax.rem(ep, 8), lax.rem(fsdp, 2) * 2 + ep // 8, fsdp // 2, core


def wave_step(i):
    return 4 + (1 - 2 * lax.rem(i, 2)) * ((i + 1) // 2)


def move_kernel(
    w_ref, had_ref, mix_ref, out_ref, scales_ref,
    w_buf, half, turned, res, sent, top, mine,
    w_sem, b_send, b_recv, a_send, a_recv, keep_sem, pair_sem, s_send, s_recv,
):
    z, x, y, c = place()
    here = y * 4 + x
    slot = z * 2 + c
    low = lax.rem(x, 2)

    barrier = pltpu.get_barrier_semaphore()
    for dz in range(8):
        for dc in range(2):
            if dz or dc:
                pl.semaphore_signal(
                    barrier, inc=1, device_id_type=MESH,
                    device_id=device(lax.rem(z + dz, 8), x, y, lax.rem(c + dc, 2)),
                )
    for o in range(1, GROUP):
        pl.semaphore_signal(
            barrier, inc=1, device_id_type=MESH,
            device_id=device(z, lax.rem(x + o % 4, 4), lax.rem(y + o // 4, 4), c),
        )

    def goes_to(i):
        return lax.rem(z + wave_step(i), 8)

    def fetch(i):
        return pltpu.make_async_copy(w_ref.at[:, goes_to(i)], w_buf.at[i], w_sem.at[i])

    @pl.loop(0, WAVES)
    def _(i):
        fetch(i).start()

    top[...] = jnp.zeros_like(top)

    def turn(i):
        fetch(i).wait()
        rows = w_buf[i].reshape(GROUP * ROWS, WIDE)
        for first in range(0, WIDE, 256):
            wide = min(256, WIDE - first)
            got = jnp.dot(
                rows[:, first : first + wide], had_ref[:wide, :wide], preferred_element_type=jnp.float32
            ) * jnp.float32(1.0 / math.sqrt(HAD))
            half[i, :, :, first : first + wide] = got.astype(jnp.bfloat16).reshape(GROUP, ROWS, wide)
        turned[i, here] = half[i, here]

    def spread(i):
        @pl.loop(1, GROUP)
        def _(o):
            to_x, to_y = lax.rem(x + lax.rem(o, 4), 4), lax.rem(y + o // 4, 4)
            pltpu.make_async_remote_copy(
                src_ref=half.at[i, to_y * 4 + to_x],
                dst_ref=turned.at[i, here],
                send_sem=b_send,
                recv_sem=b_recv.at[i],
                device_id=device(z, to_x, to_y, c),
                device_id_type=MESH,
            ).start()

    turn(0)
    pl.semaphore_wait(barrier, 30)
    spread(0)

    @pl.loop(0, WAVES)
    def _(i):
        @pl.when(i < WAVES - 1)
        def _():
            turn(i + 1)
            spread(i + 1)

        landed = turned.at[i, pl.ds(0, GROUP - 1)]
        pltpu.make_async_copy(landed, landed, b_recv.at[i]).wait()

        cells = [
            jnp.concatenate(
                [
                    turned[i, f * 2 + e, :, t * HAD : (t + 1) * HAD]
                    for f in range(8)
                    for t in range(TILES)
                ],
                axis=0,
            )
            for e in range(2)
        ]
        res[...] = jnp.dot(
            mix_ref[...], jnp.concatenate(cells, axis=1), preferred_element_type=jnp.float32
        )
        for k in range(COS):
            for e in range(2):
                best = top[e, k]
                for to_c in range(2):
                    got = res[k * ROWS + to_c * 8 : k * ROWS + to_c * 8 + 8, e * HAD : (e + 1) * HAD]
                    best = jnp.maximum(best, jnp.abs(got))
                    sent[i, to_c, e, :, k * HAD : (k + 1) * HAD] = got.astype(jnp.bfloat16)
                top[e, k] = best

        to_z = goes_to(i)

        def ship(to_c):
            pltpu.make_async_remote_copy(
                src_ref=sent.at[i, to_c],
                dst_ref=out_ref.at[slot],
                send_sem=a_send,
                recv_sem=a_recv,
                device_id=device(to_z, x, y, to_c),
                device_id_type=MESH,
            ).start()

        ship(1 - c)

        @pl.when(i < WAVES - 1)
        def _():
            ship(c)

    keep = pltpu.make_async_copy(sent.at[WAVES - 1, c], out_ref.at[slot], keep_sem)
    keep.start()

    largest = jnp.max(jnp.max(top[...], axis=2), axis=2, keepdims=True) + jnp.float32(EPS)
    diagonal = lax.broadcasted_iota(jnp.int32, (COS, HAD), 0) == lax.broadcasted_iota(
        jnp.int32, (COS, HAD), 1
    )
    lines = [
        jnp.sum(jnp.where(diagonal, largest[e], 0.0), axis=0, keepdims=True) for e in range(2)
    ]
    mine[low] = jnp.concatenate(lines + [jnp.zeros((6, HAD), jnp.float32)], axis=0)

    pair = pltpu.make_async_remote_copy(
        src_ref=mine.at[low],
        dst_ref=mine.at[low],
        send_sem=pair_sem.at[0],
        recv_sem=pair_sem.at[1],
        device_id=device(z, x + 1 - 2 * low, y, c),
        device_id_type=MESH,
    )
    pair.start()
    pair.wait()
    scales_ref[slot] = mine[...]

    @pl.loop(1, GROUP)
    def _(o):
        pltpu.make_async_remote_copy(
            src_ref=mine,
            dst_ref=scales_ref.at[slot],
            send_sem=s_send,
            recv_sem=s_recv,
            device_id=device(lax.rem(z + o // 2, 8), x, y, lax.rem(c + o, 2)),
            device_id_type=MESH,
        ).start()

    scales = scales_ref.at[pl.ds(0, GROUP - 1)]
    pltpu.make_async_copy(scales, scales, s_recv).wait()
    pltpu.make_async_copy(scales, scales, s_send).wait()
    parts = half.at[:, pl.ds(0, GROUP - 1)]
    pltpu.make_async_copy(parts, parts, b_send).wait()
    arrived = out_ref.at[pl.ds(0, GROUP - 1)]
    pltpu.make_async_copy(arrived, arrived, a_send).wait()
    pltpu.make_async_copy(arrived, arrived, a_recv).wait()
    keep.wait()


def order_kernel(order_ref, block_ref, data_ref, scales_ref, out_ref, lines_ref, got, scaled, in_sem, out_sem):
    count = out_ref.shape[0]

    def fetch(p):
        e = order_ref[p]
        return pltpu.make_async_copy(data_ref.at[lax.rem(e, 16), e // 16], got.at[p], in_sem.at[p])

    def store(p):
        return pltpu.make_async_copy(scaled.at[p], out_ref.at[p], out_sem.at[p])

    @pl.loop(0, count)
    def _(p):
        fetch(p).start()

    diagonal = lax.broadcasted_iota(jnp.int32, (COS, HAD), 0) == lax.broadcasted_iota(
        jnp.int32, (COS, HAD), 1
    )
    low = block_ref[0]

    @pl.loop(0, count)
    def _(p):
        e = order_ref[p]
        for b in range(2):
            lines_ref[p, b : b + 1, :] = scales_ref[lax.rem(e, 16), b, pl.ds(e // 16, 1), :][:, :COS]
        line = scales_ref[lax.rem(e, 16), low, pl.ds(e // 16, 1), :]
        column = jnp.sum(jnp.where(diagonal, line, 0.0), axis=1, keepdims=True)
        factor = jnp.broadcast_to(1.0 / column, (COS, HAD))
        fetch(p).wait()
        for k in range(COS):
            cell = got[p, :, k * HAD : (k + 1) * HAD].astype(jnp.float32) * factor[k : k + 1, :]
            scaled[p, :, k * HAD : (k + 1) * HAD] = cell.astype(jnp.bfloat16)
        store(p).start()

    @pl.loop(0, count)
    def _(p):
        store(p).wait()


def per_device(weights, owner_map):
    bf16, f32 = jnp.bfloat16, jnp.float32
    had = np.kron(np.eye(2, dtype=np.float32), hadamard()).astype(ml_dtypes.bfloat16)
    mix = np.kron(cosine(), np.eye(ROWS, dtype=np.float32)).astype(ml_dtypes.bfloat16)
    vmem = pl.BlockSpec(memory_space=pltpu.VMEM)
    anywhere = pl.BlockSpec(memory_space=pl.ANY)
    moved, scales = pl.pallas_call(
        move_kernel,
        out_shape=(
            jax.ShapeDtypeStruct((GROUP, 2, 8, D), bf16),
            jax.ShapeDtypeStruct((GROUP, 2, 8, HAD), f32),
        ),
        in_specs=[anywhere, vmem, vmem],
        out_specs=(anywhere, vmem),
        scratch_shapes=[
            pltpu.VMEM((WAVES, GROUP, ROWS, WIDE), bf16),
            pltpu.VMEM((WAVES, GROUP, ROWS, WIDE), bf16),
            pltpu.VMEM((WAVES, GROUP, ROWS, WIDE), bf16),
            pltpu.VMEM((COS * ROWS, 2 * HAD), f32),
            pltpu.VMEM((WAVES, 2, 2, 8, D), bf16),
            pltpu.VMEM((2, COS, 8, HAD), f32),
            pltpu.VMEM((2, 8, HAD), f32),
            pltpu.SemaphoreType.DMA((WAVES,)),
            pltpu.SemaphoreType.DMA,
            pltpu.SemaphoreType.DMA((WAVES,)),
            pltpu.SemaphoreType.DMA,
            pltpu.SemaphoreType.DMA,
            pltpu.SemaphoreType.DMA,
            pltpu.SemaphoreType.DMA((2,)),
            pltpu.SemaphoreType.DMA,
            pltpu.SemaphoreType.DMA,
        ],
        compiler_params=pltpu.CompilerParams(
            collective_id=0, has_side_effects=True, vmem_limit_bytes=48 * 2**20
        ),
        name="move",
    )(weights.reshape(GROUP, WAVES, ROWS, WIDE), jnp.asarray(had), jnp.asarray(mix))
    count = owner_map.shape[0]
    quant, lines = pl.pallas_call(
        order_kernel,
        out_shape=(
            jax.ShapeDtypeStruct((count, 8, D), bf16),
            jax.ShapeDtypeStruct((count, 2, COS), f32),
        ),
        in_specs=[
            pl.BlockSpec(memory_space=pltpu.SMEM),
            pl.BlockSpec(memory_space=pltpu.SMEM),
            anywhere,
            vmem,
        ],
        out_specs=(anywhere, vmem),
        scratch_shapes=[
            pltpu.VMEM((count, 8, D), bf16),
            pltpu.VMEM((count, 8, D), bf16),
            pltpu.SemaphoreType.DMA((count,)),
            pltpu.SemaphoreType.DMA((count,)),
        ],
        compiler_params=pltpu.CompilerParams(vmem_limit_bytes=32 * 2**20),
        name="order",
    )(positions(owner_map), (lax.axis_index("ep") // 8).reshape(1), moved, scales)
    return quant.reshape(count, 1, 8, D), lines


def solution(mesh):
    return jax.shard_map(
        per_device,
        mesh=mesh,
        in_specs=(P(("ep", "rep"), None, "fsdp"), P()),
        out_specs=(P(None, "fsdp", ("ep", "rep"), None), P(None, "fsdp", None)),
        check_vma=False,
    )
```

```python
import math

import jax
import jax.numpy as jnp
import ml_dtypes
import numpy as np
from jax import lax
from jax.experimental import pallas as pl
from jax.experimental.pallas import tpu as pltpu
from jax.sharding import PartitionSpec as P

MESH = pl.DeviceIdType.MESH
D = 7168
HAD = 128
COS = 56
WIDE = 896
TILES = WIDE // HAD
ROWS = 16
WAVES = 8
HELD = 3
GROUP = 16
EPS = 1e-06


def hadamard():
    i = np.arange(HAD)
    both = i[:, None] & i[None, :]
    ones = sum((both >> bit) & 1 for bit in range(7))
    return (1 - 2 * (ones % 2)).astype(np.float32)


def cosine():
    k = np.arange(COS, dtype=np.float64)[:, None]
    j = np.arange(COS, dtype=np.float64)[None, :]
    c = np.sqrt(2.0 / COS) * np.cos(np.pi * (2 * j + 1) * k / (2 * COS))
    c[0] *= np.sqrt(0.5)
    return c.astype(ml_dtypes.bfloat16).astype(np.float32)


def device(z, x, y, c):
    return (lax.rem(x, 2) * 8 + z, y * 2 + x // 2, c)


def place():
    ep, fsdp, core = lax.axis_index("ep"), lax.axis_index("fsdp"), lax.axis_index("rep")
    return lax.rem(ep, 8), lax.rem(fsdp, 2) * 2 + ep // 8, fsdp // 2, core


def wave_step(i):
    return 4 + (1 - 2 * lax.rem(i, 2)) * ((i + 1) // 2)


def column_of(line, mask):
    return jnp.sum(jnp.where(mask, line, 0.0), axis=1, keepdims=True)


def diagonal(rows, lanes):
    return lax.broadcasted_iota(jnp.int32, (rows, lanes), 0) == lax.broadcasted_iota(
        jnp.int32, (rows, lanes), 1
    )


def move_kernel(
    w_ref, had_hbm, mix_hbm, owner_ref, out_ref, scales_ref, order_ref,
    had_ref, mix_ref, w_buf, half, turned, res, sent, arrived, top, lines, tops, factors,
    t_sem, w_sem, p_sem, b_send, b_recv, a_send, a_recv, pair_sem, s_send, s_recv,
):
    z, x, y, c = place()
    here = y * 4 + x
    slot = z * 2 + c
    low = lax.rem(x, 2)
    across = lax.rem(z + 4, 8)

    barrier = pltpu.get_barrier_semaphore()
    for dz in range(8):
        for dc in range(2):
            if dz or dc:
                pl.semaphore_signal(
                    barrier, inc=1, device_id_type=MESH,
                    device_id=device(lax.rem(z + dz, 8), x, y, lax.rem(c + dc, 2)),
                )
    for o in range(1, GROUP):
        pl.semaphore_signal(
            barrier, inc=1, device_id_type=MESH,
            device_id=device(z, lax.rem(x + o % 4, 4), lax.rem(y + o // 4, 4), c),
        )

    def goes_to(i):
        return lax.rem(z + wave_step(i), 8)

    def fetch(i):
        return pltpu.make_async_copy(w_ref.at[:, goes_to(i)], w_buf.at[i], w_sem.at[i])

    get_had = pltpu.make_async_copy(had_hbm, had_ref, t_sem.at[0])
    get_mix = pltpu.make_async_copy(mix_hbm, mix_ref, t_sem.at[1])
    get_had.start()

    @pl.loop(0, WAVES)
    def _(i):
        fetch(i).start()

    get_mix.start()

    top[...] = jnp.zeros_like(top)

    def turn(i):
        fetch(i).wait()
        rows = w_buf[i].reshape(GROUP * ROWS, WIDE)
        for first in range(0, WIDE, 256):
            wide = min(256, WIDE - first)
            got = jnp.dot(
                rows[:, first : first + wide], had_ref[:wide, :wide], preferred_element_type=jnp.float32
            ) * jnp.float32(1.0 / math.sqrt(HAD))
            half[i, :, :, first : first + wide] = got.astype(jnp.bfloat16).reshape(GROUP, ROWS, wide)

    def spread(source, i):
        turned[i, here] = half[source, here]

        @pl.loop(1, GROUP)
        def _(o):
            to_x, to_y = lax.rem(x + lax.rem(o, 4), 4), lax.rem(y + o // 4, 4)
            pltpu.make_async_remote_copy(
                src_ref=half.at[source, to_y * 4 + to_x],
                dst_ref=turned.at[i, here],
                send_sem=b_send,
                recv_sem=b_recv.at[i],
                device_id=device(z, to_x, to_y, c),
                device_id_type=MESH,
            ).start()

    def send(i, to_z, into, to_c):
        pltpu.make_async_remote_copy(
            src_ref=sent.at[i, to_c],
            dst_ref=arrived.at[into],
            send_sem=a_send,
            recv_sem=a_recv.at[into],
            device_id=device(to_z, x, y, to_c),
            device_id_type=MESH,
        ).start()

    def ship(i, to_c):
        send(i, goes_to(i), slot, to_c)

    get_had.wait()
    turn(0)
    pl.semaphore_wait(barrier, 30)
    over = pltpu.make_async_remote_copy(
        src_ref=half.at[0],
        dst_ref=half.at[WAVES],
        send_sem=p_sem.at[0],
        recv_sem=p_sem.at[1],
        device_id=device(across, x, y, c),
        device_id_type=MESH,
    )
    over.start()
    turn(1)
    spread(1, 1)
    get_mix.wait()

    ids = (lax.broadcasted_iota(jnp.int32, (32, 32), 0), lax.broadcasted_iota(jnp.int32, (32, 32), 1))
    owner = jnp.broadcast_to(owner_ref[...], (32, 32)).astype(jnp.float32)
    other = column_of(owner, diagonal(32, 32))
    before = (owner < other) | ((owner == other) & (ids[1] < ids[0]))
    position = jnp.sum(before.astype(jnp.float32), axis=1, keepdims=True)
    chosen = jnp.where(position == ids[1].astype(jnp.float32), ids[0].astype(jnp.float32), 0.0)
    order_ref[...] = jnp.sum(chosen, axis=0, keepdims=True).astype(jnp.int32)

    @pl.loop(0, WAVES)
    def _(step):
        i = lax.rem(step + 1, WAVES)
        crossed = i == 0

        @pl.when(step < WAVES - 2)
        def _():
            turn(i + 1)
            spread(i + 1, i + 1)

        @pl.when(step == WAVES - 2)
        def _():
            over.wait()
            spread(WAVES, 0)

        landed = turned.at[i, pl.ds(0, GROUP - 1)]
        pltpu.make_async_copy(landed, landed, b_recv.at[i]).wait()

        cells = [
            jnp.concatenate(
                [
                    turned[i, f * 2 + e, :, t * HAD : (t + 1) * HAD]
                    for f in range(8)
                    for t in range(TILES)
                ],
                axis=0,
            )
            for e in range(2)
        ]
        res[...] = jnp.dot(
            mix_ref[...], jnp.concatenate(cells, axis=1), preferred_element_type=jnp.float32
        )
        which = jnp.where(crossed, 1, 0)
        for k in range(COS):
            for e in range(2):
                best = top[which, e, k]
                for to_c in range(2):
                    got = res[k * ROWS + to_c * 8 : k * ROWS + to_c * 8 + 8, e * HAD : (e + 1) * HAD]
                    best = jnp.maximum(best, jnp.abs(got))
                    sent[i, to_c, e, :, k * HAD : (k + 1) * HAD] = got.astype(jnp.bfloat16)
                top[which, e, k] = best

        @pl.when(step < HELD)
        def _():
            ship(i, 0)
            ship(i, 1)

        @pl.when(step >= WAVES - 2)
        def _():
            into = jnp.where(crossed, across * 2 + c, slot)
            send(i, z, into, 1 - c)
            pltpu.make_async_copy(sent.at[i, c], arrived.at[into], a_recv.at[into]).start()

    mask = diagonal(COS, HAD)
    rows = []
    for which in range(2):
        largest = jnp.max(jnp.max(top[which], axis=2), axis=2, keepdims=True)
        rows += [jnp.sum(jnp.where(mask, largest[e], 0.0), axis=0, keepdims=True) for e in range(2)]
    mine = jnp.concatenate(rows + [jnp.zeros((4, HAD), jnp.float32)], axis=0)
    lines[...] = mine
    tops[slot] = mine

    @pl.loop(1, GROUP)
    def _(o):
        pltpu.make_async_remote_copy(
            src_ref=lines,
            dst_ref=tops.at[slot],
            send_sem=s_send,
            recv_sem=s_recv,
            device_id=device(lax.rem(z + o // 2, 8), x, y, lax.rem(c + o, 2)),
            device_id_type=MESH,
        ).start()

    @pl.loop(HELD, WAVES - 2)
    def _(step):
        ship(step + 1, 0)
        ship(step + 1, 1)

    others = tops.at[pl.ds(0, GROUP - 1)]
    pltpu.make_async_copy(others, others, s_recv).wait()
    for e in range(2):
        crossing = jnp.concatenate([tops[8:, 2 + e, :], tops[:8, 2 + e, :]], axis=0)
        scales_ref[low, e] = jnp.maximum(tops[:, e, :], crossing) + jnp.float32(EPS)
    pair = pltpu.make_async_remote_copy(
        src_ref=scales_ref.at[low],
        dst_ref=scales_ref.at[low],
        send_sem=pair_sem.at[0],
        recv_sem=pair_sem.at[1],
        device_id=device(z, x + 1 - 2 * low, y, c),
        device_id_type=MESH,
    )
    pair.start()

    @pl.loop(0, GROUP)
    def _(s):
        for e in range(2):
            column = column_of(scales_ref[low, e, pl.ds(s, 1), :], mask)
            factors[s, e] = jnp.broadcast_to(1.0 / column, (COS, HAD))

    @pl.loop(0, GROUP)
    def _(step):
        from_z = lax.rem(z + 8 - wave_step(lax.rem(step // 2 + 7, 8)), 8)
        s = from_z * 2 + lax.rem(step, 2)
        pltpu.make_async_copy(arrived.at[s], arrived.at[s], a_recv.at[s]).wait()
        for e in range(2):
            for k in range(COS):
                cell = arrived[s, e, :, k * HAD : (k + 1) * HAD].astype(jnp.float32)
                cell = cell * factors[s, e, k : k + 1, :]
                out_ref[s, e, :, k * HAD : (k + 1) * HAD] = cell.astype(jnp.bfloat16)

    pltpu.make_async_copy(others, others, s_send).wait()
    pair.wait()
    parts = half.at[pl.ds(0, WAVES), pl.ds(0, GROUP - 1)]
    pltpu.make_async_copy(parts, parts, b_send).wait()
    shipped = arrived.at[pl.ds(0, GROUP - 2)]
    pltpu.make_async_copy(shipped, shipped, a_send).wait()


def order_kernel(order_ref, data_ref, scales_ref, out_ref, lines_ref, lines, sem, lines_sem):
    count = out_ref.shape[0]

    @pl.loop(0, count)
    def _(p):
        e = order_ref[0, p]
        pltpu.make_async_copy(data_ref.at[lax.rem(e, GROUP), e // GROUP], out_ref.at[p], sem).start()

    @pl.loop(0, count)
    def _(p):
        e = order_ref[0, p]
        for b in range(2):
            lines[p, b : b + 1, :] = scales_ref[b, e // GROUP, pl.ds(lax.rem(e, GROUP), 1), :][:, :COS]

    put = pltpu.make_async_copy(lines, lines_ref, lines_sem)
    put.start()
    pltpu.make_async_copy(out_ref, out_ref, sem).wait()
    put.wait()


def per_device(weights, owner_map):
    bf16, f32 = jnp.bfloat16, jnp.float32
    had = np.kron(np.eye(2, dtype=np.float32), hadamard()).astype(ml_dtypes.bfloat16)
    mix = np.kron(cosine(), np.eye(ROWS, dtype=np.float32)).astype(ml_dtypes.bfloat16)
    vmem = pl.BlockSpec(memory_space=pltpu.VMEM)
    smem = pl.BlockSpec(memory_space=pltpu.SMEM)
    anywhere = pl.BlockSpec(memory_space=pl.ANY)
    hbm = pl.BlockSpec(memory_space=pltpu.HBM)
    count = owner_map.shape[0]
    dma = pltpu.SemaphoreType.DMA
    moved, scales, order = pl.pallas_call(
        move_kernel,
        out_shape=(
            pltpu.VMEM((GROUP, 2, 8, D), bf16),
            pltpu.VMEM((2, 2, GROUP, HAD), f32),
            jax.ShapeDtypeStruct((1, count), jnp.int32),
        ),
        in_specs=[hbm, hbm, hbm, vmem],
        out_specs=(vmem, vmem, vmem),
        scratch_shapes=[
            pltpu.VMEM(had.shape, bf16),
            pltpu.VMEM(mix.shape, bf16),
            pltpu.VMEM((WAVES, GROUP, ROWS, WIDE), bf16),
            pltpu.VMEM((WAVES + 1, GROUP, ROWS, WIDE), bf16),
            pltpu.VMEM((WAVES, GROUP, ROWS, WIDE), bf16),
            pltpu.VMEM((COS * ROWS, 2 * HAD), f32),
            pltpu.VMEM((WAVES, 2, 2, 8, D), bf16),
            pltpu.VMEM((GROUP, 2, 8, D), bf16),
            pltpu.VMEM((2, 2, COS, 8, HAD), f32),
            pltpu.VMEM((8, HAD), f32),
            pltpu.VMEM((GROUP, 8, HAD), f32),
            pltpu.VMEM((GROUP, 2, COS, HAD), f32),
            dma((2,)),
            dma((WAVES,)),
            dma((2,)),
            dma,
            dma((WAVES,)),
            dma,
            dma((GROUP,)),
            dma((2,)),
            dma,
            dma,
        ],
        compiler_params=pltpu.CompilerParams(
            collective_id=0, has_side_effects=True, vmem_limit_bytes=52 * 2**20
        ),
        name="move",
    )(
        weights.reshape(GROUP, WAVES, ROWS, WIDE),
        jnp.asarray(had),
        jnp.asarray(mix),
        owner_map.reshape(1, count),
    )
    quant, lines = pl.pallas_call(
        order_kernel,
        out_shape=(
            jax.ShapeDtypeStruct((count, 8, D), bf16),
            jax.ShapeDtypeStruct((count, 2, COS), f32),
        ),
        in_specs=[smem, vmem, vmem],
        out_specs=(anywhere, anywhere),
        scratch_shapes=[pltpu.VMEM((count, 2, COS), f32), dma, dma],
        compiler_params=pltpu.CompilerParams(vmem_limit_bytes=8 * 2**20),
        name="order",
    )(order, moved, scales)
    return quant.reshape(count, 1, 8, D), lines


def solution(mesh):
    return jax.shard_map(
        per_device,
        mesh=mesh,
        in_specs=(P(("ep", "rep"), None, "fsdp"), P()),
        out_specs=(P(None, "fsdp", ("ep", "rep"), None), P(None, "fsdp", None)),
        check_vma=False,
    )
```

```python
import math

import jax
import jax.numpy as jnp
import ml_dtypes
import numpy as np
from jax import lax
from jax.experimental import pallas as pl
from jax.experimental.pallas import tpu as pltpu
from jax.sharding import PartitionSpec as P

MESH = pl.DeviceIdType.MESH
D = 7168
HAD = 128
COS = 56
WIDE = 896
TILES = WIDE // HAD
ROWS = 16
WAVES = 8
HELD = 2
LAST = 4
GROUP = 16
EPS = 1e-06


def hadamard():
    i = np.arange(HAD)
    both = i[:, None] & i[None, :]
    ones = sum((both >> bit) & 1 for bit in range(7))
    return (1 - 2 * (ones % 2)).astype(np.float32)


def cosine():
    k = np.arange(COS, dtype=np.float64)[:, None]
    j = np.arange(COS, dtype=np.float64)[None, :]
    c = np.sqrt(2.0 / COS) * np.cos(np.pi * (2 * j + 1) * k / (2 * COS))
    c[0] *= np.sqrt(0.5)
    return c.astype(ml_dtypes.bfloat16).astype(np.float32)


def device(z, x, y, c):
    return (lax.rem(x, 2) * 8 + z, y * 2 + x // 2, c)


def place():
    ep, fsdp, core = lax.axis_index("ep"), lax.axis_index("fsdp"), lax.axis_index("rep")
    return lax.rem(ep, 8), lax.rem(fsdp, 2) * 2 + ep // 8, fsdp // 2, core


def wave_step(i):
    return 4 + (1 - 2 * lax.rem(i, 2)) * ((i + 1) // 2)


def column_of(line, mask):
    return jnp.sum(jnp.where(mask, line, 0.0), axis=1, keepdims=True)


def diagonal(rows, lanes):
    return lax.broadcasted_iota(jnp.int32, (rows, lanes), 0) == lax.broadcasted_iota(
        jnp.int32, (rows, lanes), 1
    )


def move_kernel(
    w_ref, had_hbm, mix_hbm, owner_ref, out_ref, scales_ref, order_ref,
    had_ref, mix_ref, w_buf, half, turned, res, sent, arrived, top, lines, tops, factors,
    t_sem, w_sem, p_sem, b_send, b_recv, a_send, a_recv, pair_sem, s_send, s_recv,
):
    z, x, y, c = place()
    here = y * 4 + x
    slot = z * 2 + c
    low = lax.rem(x, 2)
    across = lax.rem(z + 4, 8)

    def goes_to(i):
        return lax.rem(z + wave_step(i), 8)

    def fetch(i):
        return pltpu.make_async_copy(w_ref.at[:, goes_to(i)], w_buf.at[i], w_sem.at[i])

    get_had = pltpu.make_async_copy(had_hbm, had_ref, t_sem.at[0])
    get_mix = pltpu.make_async_copy(mix_hbm, mix_ref, t_sem.at[1])
    get_had.start()
    fetch(0).start()

    barrier = pltpu.get_barrier_semaphore()
    for dz in (4, 3, 5, 2, 6, 1, 7, 0):
        for dc in range(2):
            if dz or dc:
                pl.semaphore_signal(
                    barrier, inc=1, device_id_type=MESH,
                    device_id=device(lax.rem(z + dz, 8), x, y, lax.rem(c + dc, 2)),
                )
    for o in range(1, GROUP):
        pl.semaphore_signal(
            barrier, inc=1, device_id_type=MESH,
            device_id=device(z, lax.rem(x + o % 4, 4), lax.rem(y + o // 4, 4), c),
        )

    @pl.loop(1, WAVES)
    def _(i):
        fetch(i).start()

    get_mix.start()

    def turn(i):
        fetch(i).wait()
        rows = w_buf[i].reshape(GROUP * ROWS, WIDE)
        for first in range(0, WIDE, 256):
            wide = min(256, WIDE - first)
            got = jnp.dot(
                rows[:, first : first + wide], had_ref[:wide, :wide], preferred_element_type=jnp.float32
            ) * jnp.float32(1.0 / math.sqrt(HAD))
            half[i, :, :, first : first + wide] = got.astype(jnp.bfloat16).reshape(GROUP, ROWS, wide)

    def spread(source, i):
        turned[i, here] = half[source, here]

        @pl.loop(1, GROUP)
        def _(o):
            to_x, to_y = lax.rem(x + lax.rem(o, 4), 4), lax.rem(y + o // 4, 4)
            pltpu.make_async_remote_copy(
                src_ref=half.at[source, to_y * 4 + to_x],
                dst_ref=turned.at[i, here],
                send_sem=b_send,
                recv_sem=b_recv.at[i],
                device_id=device(z, to_x, to_y, c),
                device_id_type=MESH,
            ).start()

    def send(i, to_z, into, to_c):
        pltpu.make_async_remote_copy(
            src_ref=sent.at[i, to_c],
            dst_ref=arrived.at[into],
            send_sem=a_send,
            recv_sem=a_recv.at[into],
            device_id=device(to_z, x, y, to_c),
            device_id_type=MESH,
        ).start()

    def ship(i, to_c):
        send(i, goes_to(i), slot, to_c)

    get_had.wait()
    turn(0)
    pl.semaphore_wait(barrier, 30)
    over = pltpu.make_async_remote_copy(
        src_ref=half.at[0],
        dst_ref=half.at[WAVES],
        send_sem=p_sem.at[0],
        recv_sem=p_sem.at[1],
        device_id=device(across, x, y, c),
        device_id_type=MESH,
    )
    over.start()
    turn(1)
    spread(1, 1)
    top[...] = jnp.zeros_like(top)
    get_mix.wait()

    ids = (lax.broadcasted_iota(jnp.int32, (32, 32), 0), lax.broadcasted_iota(jnp.int32, (32, 32), 1))
    owner = jnp.broadcast_to(owner_ref[...], (32, 32)).astype(jnp.float32)
    other = column_of(owner, diagonal(32, 32))
    before = (owner < other) | ((owner == other) & (ids[1] < ids[0]))
    position = jnp.sum(before.astype(jnp.float32), axis=1, keepdims=True)
    chosen = jnp.where(position == ids[1].astype(jnp.float32), ids[0].astype(jnp.float32), 0.0)
    order_ref[...] = jnp.sum(chosen, axis=0, keepdims=True).astype(jnp.int32)

    @pl.loop(0, WAVES)
    def _(step):
        i = lax.rem(step + 1, WAVES)
        crossed = i == 0

        @pl.when(step < WAVES - 2)
        def _():
            turn(i + 1)
            spread(i + 1, i + 1)

        @pl.when(step == WAVES - 2)
        def _():
            over.wait()
            spread(WAVES, 0)

        landed = turned.at[i, pl.ds(0, GROUP - 1)]
        pltpu.make_async_copy(landed, landed, b_recv.at[i]).wait()

        cells = [
            jnp.concatenate(
                [
                    turned[i, f * 2 + e, :, t * HAD : (t + 1) * HAD]
                    for f in range(8)
                    for t in range(TILES)
                ],
                axis=0,
            )
            for e in range(2)
        ]
        res[...] = jnp.dot(
            mix_ref[...], jnp.concatenate(cells, axis=1), preferred_element_type=jnp.float32
        )
        which = jnp.where(crossed, 1, 0)
        for k in range(COS):
            for e in range(2):
                best = top[which, e, k]
                for to_c in range(2):
                    got = res[k * ROWS + to_c * 8 : k * ROWS + to_c * 8 + 8, e * HAD : (e + 1) * HAD]
                    best = jnp.maximum(best, jnp.abs(got))
                    sent[i, to_c, e, :, k * HAD : (k + 1) * HAD] = got.astype(jnp.bfloat16)
                top[which, e, k] = best

        @pl.when(step < HELD)
        def _():
            ship(i, 0)
            ship(i, 1)

        @pl.when(step >= WAVES - 2)
        def _():
            into = jnp.where(crossed, across * 2 + c, slot)
            send(i, z, into, 1 - c)
            pltpu.make_async_copy(sent.at[i, c], arrived.at[into], a_recv.at[into]).start()

    mask = diagonal(COS, HAD)
    rows = []
    for which in range(2):
        largest = jnp.max(jnp.max(top[which], axis=2), axis=2, keepdims=True)
        rows += [jnp.sum(jnp.where(mask, largest[e], 0.0), axis=0, keepdims=True) for e in range(2)]
    mine = jnp.concatenate(rows + [jnp.zeros((4, HAD), jnp.float32)], axis=0)
    lines[...] = mine
    tops[slot] = mine

    @pl.loop(1, GROUP)
    def _(o):
        pltpu.make_async_remote_copy(
            src_ref=lines,
            dst_ref=tops.at[slot],
            send_sem=s_send,
            recv_sem=s_recv,
            device_id=device(lax.rem(z + o // 2, 8), x, y, lax.rem(c + o, 2)),
            device_id_type=MESH,
        ).start()

    @pl.loop(HELD, LAST)
    def _(step):
        ship(step + 1, 0)
        ship(step + 1, 1)

    others = tops.at[pl.ds(0, GROUP - 1)]
    pltpu.make_async_copy(others, others, s_recv).wait()
    for e in range(2):
        crossing = jnp.concatenate([tops[8:, 2 + e, :], tops[:8, 2 + e, :]], axis=0)
        scales_ref[low, e] = jnp.maximum(tops[:, e, :], crossing) + jnp.float32(EPS)
    pair = pltpu.make_async_remote_copy(
        src_ref=scales_ref.at[low],
        dst_ref=scales_ref.at[low],
        send_sem=pair_sem.at[0],
        recv_sem=pair_sem.at[1],
        device_id=device(z, x + 1 - 2 * low, y, c),
        device_id_type=MESH,
    )
    pair.start()

    @pl.loop(LAST, WAVES - 2)
    def _(step):
        ship(step + 1, 0)
        ship(step + 1, 1)

    @pl.loop(0, GROUP)
    def _(s):
        for e in range(2):
            column = column_of(scales_ref[low, e, pl.ds(s, 1), :], mask)
            factors[s, e] = jnp.broadcast_to(1.0 / column, (COS, HAD))

    @pl.loop(0, GROUP)
    def _(step):
        from_z = lax.rem(z + 8 - wave_step(lax.rem(step // 2 + 7, 8)), 8)
        s = from_z * 2 + lax.rem(step, 2)
        pltpu.make_async_copy(arrived.at[s], arrived.at[s], a_recv.at[s]).wait()
        for e in range(2):
            for k in range(COS):
                cell = arrived[s, e, :, k * HAD : (k + 1) * HAD].astype(jnp.float32)
                cell = cell * factors[s, e, k : k + 1, :]
                out_ref[s, e, :, k * HAD : (k + 1) * HAD] = cell.astype(jnp.bfloat16)

    pltpu.make_async_copy(others, others, s_send).wait()
    pair.wait()
    parts = half.at[pl.ds(0, WAVES), pl.ds(0, GROUP - 1)]
    pltpu.make_async_copy(parts, parts, b_send).wait()
    shipped = arrived.at[pl.ds(0, GROUP - 2)]
    pltpu.make_async_copy(shipped, shipped, a_send).wait()


def order_kernel(
    order_vmem, data_ref, scales_ref, out_ref, lines_ref, order_ref, lines, sem, lines_sem, order_sem
):
    count = out_ref.shape[0]
    get_order = pltpu.make_async_copy(order_vmem, order_ref, order_sem)
    get_order.start()
    get_order.wait()

    @pl.loop(0, count)
    def _(p):
        e = order_ref[0, p]
        pltpu.make_async_copy(data_ref.at[lax.rem(e, GROUP), e // GROUP], out_ref.at[p], sem).start()

    @pl.loop(0, count)
    def _(p):
        e = order_ref[0, p]
        for b in range(2):
            lines[p, b : b + 1, :] = scales_ref[b, e // GROUP, pl.ds(lax.rem(e, GROUP), 1), :][:, :COS]

    put = pltpu.make_async_copy(lines, lines_ref, lines_sem)
    put.start()
    pltpu.make_async_copy(out_ref, out_ref, sem).wait()
    put.wait()


def per_device(weights, owner_map):
    bf16, f32 = jnp.bfloat16, jnp.float32
    had = np.kron(np.eye(2, dtype=np.float32), hadamard()).astype(ml_dtypes.bfloat16)
    mix = np.kron(cosine(), np.eye(ROWS, dtype=np.float32)).astype(ml_dtypes.bfloat16)
    vmem = pl.BlockSpec(memory_space=pltpu.VMEM)
    anywhere = pl.BlockSpec(memory_space=pl.ANY)
    hbm = pl.BlockSpec(memory_space=pltpu.HBM)
    count = owner_map.shape[0]
    dma = pltpu.SemaphoreType.DMA
    moved, scales, order = pl.pallas_call(
        move_kernel,
        out_shape=(
            pltpu.VMEM((GROUP, 2, 8, D), bf16),
            pltpu.VMEM((2, 2, GROUP, HAD), f32),
            pltpu.VMEM((1, count), jnp.int32),
        ),
        in_specs=[hbm, hbm, hbm, vmem],
        out_specs=(vmem, vmem, vmem),
        scratch_shapes=[
            pltpu.VMEM(had.shape, bf16),
            pltpu.VMEM(mix.shape, bf16),
            pltpu.VMEM((WAVES, GROUP, ROWS, WIDE), bf16),
            pltpu.VMEM((WAVES + 1, GROUP, ROWS, WIDE), bf16),
            pltpu.VMEM((WAVES, GROUP, ROWS, WIDE), bf16),
            pltpu.VMEM((COS * ROWS, 2 * HAD), f32),
            pltpu.VMEM((WAVES, 2, 2, 8, D), bf16),
            pltpu.VMEM((GROUP, 2, 8, D), bf16),
            pltpu.VMEM((2, 2, COS, 8, HAD), f32),
            pltpu.VMEM((8, HAD), f32),
            pltpu.VMEM((GROUP, 8, HAD), f32),
            pltpu.VMEM((GROUP, 2, COS, HAD), f32),
            dma((2,)),
            dma((WAVES,)),
            dma((2,)),
            dma,
            dma((WAVES,)),
            dma,
            dma((GROUP,)),
            dma((2,)),
            dma,
            dma,
        ],
        compiler_params=pltpu.CompilerParams(
            collective_id=0, has_side_effects=True, vmem_limit_bytes=52 * 2**20
        ),
        name="move",
    )(
        weights.reshape(GROUP, WAVES, ROWS, WIDE),
        jnp.asarray(had),
        jnp.asarray(mix),
        owner_map.reshape(1, count),
    )
    quant, lines = pl.pallas_call(
        order_kernel,
        out_shape=(
            jax.ShapeDtypeStruct((count, 8, D), bf16),
            jax.ShapeDtypeStruct((count, 2, COS), f32),
        ),
        in_specs=[vmem, vmem, vmem],
        out_specs=(anywhere, anywhere),
        scratch_shapes=[
            pltpu.SMEM((1, count), jnp.int32),
            pltpu.VMEM((count, 2, COS), f32),
            dma,
            dma,
            dma,
        ],
        compiler_params=pltpu.CompilerParams(vmem_limit_bytes=8 * 2**20),
        name="order",
    )(order, moved, scales)
    return quant.reshape(count, 1, 8, D), lines


def solution(mesh):
    return jax.shard_map(
        per_device,
        mesh=mesh,
        in_specs=(P(("ep", "rep"), None, "fsdp"), P()),
        out_specs=(P(None, "fsdp", ("ep", "rep"), None), P(None, "fsdp", None)),
        check_vma=False,
    )
```

```python
import math

import jax
import jax.numpy as jnp
import ml_dtypes
import numpy as np
from jax import lax
from jax.experimental import pallas as pl
from jax.experimental.pallas import tpu as pltpu
from jax.sharding import PartitionSpec as P

MESH = pl.DeviceIdType.MESH
D = 7168
HAD = 128
COS = 56
WIDE = 896
TILES = WIDE // HAD
ROWS = 16
WAVES = 8
HELD = 2
LAST = 4
GROUP = 16
EPS = 1e-06


def hadamard():
    i = np.arange(HAD)
    both = i[:, None] & i[None, :]
    ones = sum((both >> bit) & 1 for bit in range(7))
    return (1 - 2 * (ones % 2)).astype(np.float32)


def cosine():
    k = np.arange(COS, dtype=np.float64)[:, None]
    j = np.arange(COS, dtype=np.float64)[None, :]
    c = np.sqrt(2.0 / COS) * np.cos(np.pi * (2 * j + 1) * k / (2 * COS))
    c[0] *= np.sqrt(0.5)
    return c.astype(ml_dtypes.bfloat16).astype(np.float32)


def device(z, x, y, c):
    return (lax.rem(x, 2) * 8 + z, y * 2 + x // 2, c)


def place():
    ep, fsdp, core = lax.axis_index("ep"), lax.axis_index("fsdp"), lax.axis_index("rep")
    return lax.rem(ep, 8), lax.rem(fsdp, 2) * 2 + ep // 8, fsdp // 2, core


def wave_step(i):
    return 4 + (1 - 2 * lax.rem(i, 2)) * ((i + 1) // 2)


def column_of(line, mask):
    return jnp.sum(jnp.where(mask, line, 0.0), axis=1, keepdims=True)


def diagonal(rows, lanes):
    return lax.broadcasted_iota(jnp.int32, (rows, lanes), 0) == lax.broadcasted_iota(
        jnp.int32, (rows, lanes), 1
    )


def move_kernel(
    w_ref, had_hbm, mix_hbm, owner_ref, out_ref, scales_ref, order_ref,
    had_ref, mix_ref, w_buf, half, turned, res, sent, arrived, top, lines, tops, factors,
    t_sem, w_sem, p_sem, b_send, b_recv, a_send, a_recv, pair_sem, s_send, s_recv,
):
    z, x, y, c = place()
    here = y * 4 + x
    slot = z * 2 + c
    low = lax.rem(x, 2)
    across = lax.rem(z + 4, 8)

    def goes_to(i):
        return lax.rem(z + wave_step(i), 8)

    def fetch(i):
        return pltpu.make_async_copy(w_ref.at[:, goes_to(i)], w_buf.at[i], w_sem.at[i])

    get_had = pltpu.make_async_copy(had_hbm, had_ref, t_sem.at[0])
    get_mix = pltpu.make_async_copy(mix_hbm, mix_ref, t_sem.at[1])
    get_had.start()
    fetch(0).start()

    barrier = pltpu.get_barrier_semaphore()
    for dz in (4, 3, 5, 2, 6, 1, 7, 0):
        for dc in range(2):
            if dz or dc:
                pl.semaphore_signal(
                    barrier, inc=1, device_id_type=MESH,
                    device_id=device(lax.rem(z + dz, 8), x, y, lax.rem(c + dc, 2)),
                )
    for o in range(1, GROUP):
        pl.semaphore_signal(
            barrier, inc=1, device_id_type=MESH,
            device_id=device(z, lax.rem(x + o % 4, 4), lax.rem(y + o // 4, 4), c),
        )

    @pl.loop(1, WAVES)
    def _(i):
        fetch(i).start()

    get_mix.start()

    def turn(i):
        fetch(i).wait()
        rows = w_buf[i].reshape(GROUP * ROWS, WIDE)
        for first in range(0, WIDE, 256):
            wide = min(256, WIDE - first)
            got = jnp.dot(
                rows[:, first : first + wide], had_ref[:wide, :wide], preferred_element_type=jnp.float32
            ) * jnp.float32(1.0 / math.sqrt(HAD))
            half[i, :, :, first : first + wide] = got.astype(jnp.bfloat16).reshape(GROUP, ROWS, wide)

    def spread(source, i):
        turned[i, here] = half[source, here]

        @pl.loop(1, GROUP)
        def _(o):
            to_x, to_y = lax.rem(x + lax.rem(o, 4), 4), lax.rem(y + o // 4, 4)
            pltpu.make_async_remote_copy(
                src_ref=half.at[source, to_y * 4 + to_x],
                dst_ref=turned.at[i, here],
                send_sem=b_send,
                recv_sem=b_recv.at[i],
                device_id=device(z, to_x, to_y, c),
                device_id_type=MESH,
            ).start()

    def send(i, to_z, into, to_c):
        pltpu.make_async_remote_copy(
            src_ref=sent.at[i, to_c],
            dst_ref=arrived.at[into],
            send_sem=a_send,
            recv_sem=a_recv.at[into],
            device_id=device(to_z, x, y, to_c),
            device_id_type=MESH,
        ).start()

    def ship(i, to_c):
        send(i, goes_to(i), slot, to_c)

    get_had.wait()
    turn(0)
    pl.semaphore_wait(barrier, 30)
    over = pltpu.make_async_remote_copy(
        src_ref=half.at[0],
        dst_ref=half.at[WAVES],
        send_sem=p_sem.at[0],
        recv_sem=p_sem.at[1],
        device_id=device(across, x, y, c),
        device_id_type=MESH,
    )
    over.start()
    turn(1)
    spread(1, 1)
    top[...] = jnp.zeros_like(top)
    get_mix.wait()

    ids = (lax.broadcasted_iota(jnp.int32, (32, 32), 0), lax.broadcasted_iota(jnp.int32, (32, 32), 1))
    owner = jnp.broadcast_to(owner_ref[...], (32, 32)).astype(jnp.float32)
    other = column_of(owner, diagonal(32, 32))
    before = (owner < other) | ((owner == other) & (ids[1] < ids[0]))
    position = jnp.sum(before.astype(jnp.float32), axis=1, keepdims=True)
    chosen = jnp.where(position == ids[1].astype(jnp.float32), ids[0].astype(jnp.float32), 0.0)
    order_ref[...] = jnp.sum(chosen, axis=0, keepdims=True).astype(jnp.int32)

    @pl.loop(0, WAVES)
    def _(step):
        i = lax.rem(step + 1, WAVES)
        crossed = i == 0

        @pl.when(step < WAVES - 2)
        def _():
            turn(i + 1)
            spread(i + 1, i + 1)

        @pl.when(step == WAVES - 2)
        def _():
            over.wait()
            spread(WAVES, 0)

        landed = turned.at[i, pl.ds(0, GROUP - 1)]
        pltpu.make_async_copy(landed, landed, b_recv.at[i]).wait()

        cells = [
            jnp.concatenate(
                [
                    turned[i, f * 2 + e, :, t * HAD : (t + 1) * HAD]
                    for f in range(8)
                    for t in range(TILES)
                ],
                axis=0,
            )
            for e in range(2)
        ]
        res[...] = jnp.dot(
            mix_ref[...], jnp.concatenate(cells, axis=1), preferred_element_type=jnp.float32
        )
        which = jnp.where(crossed, 1, 0)
        for k in range(COS):
            for e in range(2):
                best = top[which, e, k]
                for to_c in range(2):
                    got = res[k * ROWS + to_c * 8 : k * ROWS + to_c * 8 + 8, e * HAD : (e + 1) * HAD]
                    best = jnp.maximum(best, jnp.abs(got))
                    sent[i, to_c, e, :, k * HAD : (k + 1) * HAD] = got.astype(jnp.bfloat16)
                top[which, e, k] = best

        @pl.when(step < HELD)
        def _():
            ship(i, 1)
            ship(i, 0)

        @pl.when(step >= WAVES - 2)
        def _():
            into = jnp.where(crossed, across * 2 + c, slot)
            send(i, z, into, 1 - c)
            pltpu.make_async_copy(sent.at[i, c], arrived.at[into], a_recv.at[into]).start()

    mask = diagonal(COS, HAD)
    rows = []
    for which in range(2):
        largest = jnp.max(jnp.max(top[which], axis=2), axis=2, keepdims=True)
        rows += [jnp.sum(jnp.where(mask, largest[e], 0.0), axis=0, keepdims=True) for e in range(2)]
    mine = jnp.concatenate(rows + [jnp.zeros((4, HAD), jnp.float32)], axis=0)
    lines[...] = mine
    tops[slot] = mine

    @pl.loop(1, GROUP)
    def _(o):
        pltpu.make_async_remote_copy(
            src_ref=lines,
            dst_ref=tops.at[slot],
            send_sem=s_send,
            recv_sem=s_recv,
            device_id=device(lax.rem(z + o // 2, 8), x, y, lax.rem(c + o, 2)),
            device_id_type=MESH,
        ).start()

    @pl.loop(HELD, LAST)
    def _(step):
        ship(step + 1, 1)
        ship(step + 1, 0)

    others = tops.at[pl.ds(0, GROUP - 1)]
    pltpu.make_async_copy(others, others, s_recv).wait()
    for e in range(2):
        crossing = jnp.concatenate([tops[8:, 2 + e, :], tops[:8, 2 + e, :]], axis=0)
        scales_ref[low, e] = jnp.maximum(tops[:, e, :], crossing) + jnp.float32(EPS)
    pair = pltpu.make_async_remote_copy(
        src_ref=scales_ref.at[low],
        dst_ref=scales_ref.at[low],
        send_sem=pair_sem.at[0],
        recv_sem=pair_sem.at[1],
        device_id=device(z, x + 1 - 2 * low, y, c),
        device_id_type=MESH,
    )
    pair.start()

    @pl.loop(LAST, WAVES - 2)
    def _(step):
        ship(step + 1, 1)
        ship(step + 1, 0)

    @pl.loop(0, GROUP)
    def _(s):
        for e in range(2):
            column = column_of(scales_ref[low, e, pl.ds(s, 1), :], mask)
            factors[s, e] = jnp.broadcast_to(1.0 / column, (COS, HAD))

    @pl.loop(0, GROUP)
    def _(step):
        from_z = lax.rem(z + 8 - wave_step(lax.rem(step // 2 + 7, 8)), 8)
        s = from_z * 2 + lax.rem(step, 2)
        pltpu.make_async_copy(arrived.at[s], arrived.at[s], a_recv.at[s]).wait()
        for e in range(2):
            for k in range(COS):
                cell = arrived[s, e, :, k * HAD : (k + 1) * HAD].astype(jnp.float32)
                cell = cell * factors[s, e, k : k + 1, :]
                out_ref[s, e, :, k * HAD : (k + 1) * HAD] = cell.astype(jnp.bfloat16)

    pltpu.make_async_copy(others, others, s_send).wait()
    pair.wait()
    parts = half.at[pl.ds(0, WAVES), pl.ds(0, GROUP - 1)]
    pltpu.make_async_copy(parts, parts, b_send).wait()
    shipped = arrived.at[pl.ds(0, GROUP - 2)]
    pltpu.make_async_copy(shipped, shipped, a_send).wait()


def order_kernel(
    order_vmem, data_ref, scales_ref, out_ref, lines_ref, order_ref, lines, sem, lines_sem, order_sem
):
    count = out_ref.shape[0]
    get_order = pltpu.make_async_copy(order_vmem, order_ref, order_sem)
    get_order.start()
    get_order.wait()

    @pl.loop(0, count)
    def _(p):
        e = order_ref[0, p]
        pltpu.make_async_copy(data_ref.at[lax.rem(e, GROUP), e // GROUP], out_ref.at[p], sem).start()

    @pl.loop(0, count)
    def _(p):
        e = order_ref[0, p]
        for b in range(2):
            lines[p, b : b + 1, :] = scales_ref[b, e // GROUP, pl.ds(lax.rem(e, GROUP), 1), :][:, :COS]

    put = pltpu.make_async_copy(lines, lines_ref, lines_sem)
    put.start()
    pltpu.make_async_copy(out_ref, out_ref, sem).wait()
    put.wait()


def per_device(weights, owner_map):
    bf16, f32 = jnp.bfloat16, jnp.float32
    had = np.kron(np.eye(2, dtype=np.float32), hadamard()).astype(ml_dtypes.bfloat16)
    mix = np.kron(cosine(), np.eye(ROWS, dtype=np.float32)).astype(ml_dtypes.bfloat16)
    vmem = pl.BlockSpec(memory_space=pltpu.VMEM)
    anywhere = pl.BlockSpec(memory_space=pl.ANY)
    hbm = pl.BlockSpec(memory_space=pltpu.HBM)
    count = owner_map.shape[0]
    dma = pltpu.SemaphoreType.DMA
    moved, scales, order = pl.pallas_call(
        move_kernel,
        out_shape=(
            pltpu.VMEM((GROUP, 2, 8, D), bf16),
            pltpu.VMEM((2, 2, GROUP, HAD), f32),
            pltpu.VMEM((1, count), jnp.int32),
        ),
        in_specs=[hbm, hbm, hbm, vmem],
        out_specs=(vmem, vmem, vmem),
        scratch_shapes=[
            pltpu.VMEM(had.shape, bf16),
            pltpu.VMEM(mix.shape, bf16),
            pltpu.VMEM((WAVES, GROUP, ROWS, WIDE), bf16),
            pltpu.VMEM((WAVES + 1, GROUP, ROWS, WIDE), bf16),
            pltpu.VMEM((WAVES, GROUP, ROWS, WIDE), bf16),
            pltpu.VMEM((COS * ROWS, 2 * HAD), f32),
            pltpu.VMEM((WAVES, 2, 2, 8, D), bf16),
            pltpu.VMEM((GROUP, 2, 8, D), bf16),
            pltpu.VMEM((2, 2, COS, 8, HAD), f32),
            pltpu.VMEM((8, HAD), f32),
            pltpu.VMEM((GROUP, 8, HAD), f32),
            pltpu.VMEM((GROUP, 2, COS, HAD), f32),
            dma((2,)),
            dma((WAVES,)),
            dma((2,)),
            dma,
            dma((WAVES,)),
            dma,
            dma((GROUP,)),
            dma((2,)),
            dma,
            dma,
        ],
        compiler_params=pltpu.CompilerParams(
            collective_id=0, has_side_effects=True, vmem_limit_bytes=52 * 2**20
        ),
        name="move",
    )(
        weights.reshape(GROUP, WAVES, ROWS, WIDE),
        jnp.asarray(had),
        jnp.asarray(mix),
        owner_map.reshape(1, count),
    )
    quant, lines = pl.pallas_call(
        order_kernel,
        out_shape=(
            jax.ShapeDtypeStruct((count, 8, D), bf16),
            jax.ShapeDtypeStruct((count, 2, COS), f32),
        ),
        in_specs=[vmem, vmem, vmem],
        out_specs=(anywhere, anywhere),
        scratch_shapes=[
            pltpu.SMEM((1, count), jnp.int32),
            pltpu.VMEM((count, 2, COS), f32),
            dma,
            dma,
            dma,
        ],
        compiler_params=pltpu.CompilerParams(vmem_limit_bytes=8 * 2**20),
        name="order",
    )(order, moved, scales)
    return quant.reshape(count, 1, 8, D), lines


def solution(mesh):
    return jax.shard_map(
        per_device,
        mesh=mesh,
        in_specs=(P(("ep", "rep"), None, "fsdp"), P()),
        out_specs=(P(None, "fsdp", ("ep", "rep"), None), P(None, "fsdp", None)),
        check_vma=False,
    )
```

```python
import math

import jax
import jax.numpy as jnp
import ml_dtypes
import numpy as np
from jax import lax
from jax.experimental import pallas as pl
from jax.experimental.pallas import tpu as pltpu
from jax.sharding import PartitionSpec as P

MESH = pl.DeviceIdType.MESH
D = 7168
HAD = 128
COS = 56
WIDE = 896
TILES = WIDE // HAD
ROWS = 16
WAVES = 8
HELD = 2
LAST = 4
GROUP = 16
EPS = 1e-06


def hadamard():
    i = np.arange(HAD)
    both = i[:, None] & i[None, :]
    ones = sum((both >> bit) & 1 for bit in range(7))
    return (1 - 2 * (ones % 2)).astype(np.float32)


def cosine():
    k = np.arange(COS, dtype=np.float64)[:, None]
    j = np.arange(COS, dtype=np.float64)[None, :]
    c = np.sqrt(2.0 / COS) * np.cos(np.pi * (2 * j + 1) * k / (2 * COS))
    c[0] *= np.sqrt(0.5)
    return c.astype(ml_dtypes.bfloat16).astype(np.float32)


def device(z, x, y, c):
    return (lax.rem(x, 2) * 8 + z, y * 2 + x // 2, c)


def place():
    ep, fsdp, core = lax.axis_index("ep"), lax.axis_index("fsdp"), lax.axis_index("rep")
    return lax.rem(ep, 8), lax.rem(fsdp, 2) * 2 + ep // 8, fsdp // 2, core


def wave_step(i):
    return 4 + (1 - 2 * lax.rem(i, 2)) * ((i + 1) // 2)


def column_of(line, mask):
    return jnp.sum(jnp.where(mask, line, 0.0), axis=1, keepdims=True)


def diagonal(rows, lanes):
    return lax.broadcasted_iota(jnp.int32, (rows, lanes), 0) == lax.broadcasted_iota(
        jnp.int32, (rows, lanes), 1
    )


def move_kernel(
    w_ref, had_hbm, mix_hbm, owner_ref, out_ref, scales_ref, order_ref,
    had_ref, mix_ref, w_buf, half, turned, res, sent, arrived, top, lines, tops, factors, order_vmem,
    t_sem, w_sem, p_sem, b_send, b_recv, a_send, a_recv, pair_sem, s_send, s_recv,
):
    z, x, y, c = place()
    here = y * 4 + x
    slot = z * 2 + c
    low = lax.rem(x, 2)
    across = lax.rem(z + 4, 8)

    def goes_to(i):
        return lax.rem(z + wave_step(i), 8)

    def fetch(i):
        return pltpu.make_async_copy(w_ref.at[:, goes_to(i)], w_buf.at[i], w_sem.at[i])

    get_had = pltpu.make_async_copy(had_hbm, had_ref, t_sem.at[0])
    get_mix = pltpu.make_async_copy(mix_hbm, mix_ref, t_sem.at[1])
    get_had.start()
    fetch(0).start()

    barrier = pltpu.get_barrier_semaphore()
    for dz in (4, 3, 5, 2, 6, 1, 7, 0):
        for dc in range(2):
            if dz or dc:
                pl.semaphore_signal(
                    barrier, inc=1, device_id_type=MESH,
                    device_id=device(lax.rem(z + dz, 8), x, y, lax.rem(c + dc, 2)),
                )
    for o in range(1, GROUP):
        pl.semaphore_signal(
            barrier, inc=1, device_id_type=MESH,
            device_id=device(z, lax.rem(x + o % 4, 4), lax.rem(y + o // 4, 4), c),
        )

    @pl.loop(1, WAVES)
    def _(i):
        fetch(i).start()

    get_mix.start()

    def turn(i):
        fetch(i).wait()
        rows = w_buf[i].reshape(GROUP * ROWS, WIDE)
        for first in range(0, WIDE, 256):
            wide = min(256, WIDE - first)
            got = jnp.dot(
                rows[:, first : first + wide], had_ref[:wide, :wide], preferred_element_type=jnp.float32
            ) * jnp.float32(1.0 / math.sqrt(HAD))
            half[i, :, :, first : first + wide] = got.astype(jnp.bfloat16).reshape(GROUP, ROWS, wide)

    def spread(source, i):
        turned[i, here] = half[source, here]

        @pl.loop(1, GROUP)
        def _(o):
            to_x, to_y = lax.rem(x + lax.rem(o, 4), 4), lax.rem(y + o // 4, 4)
            pltpu.make_async_remote_copy(
                src_ref=half.at[source, to_y * 4 + to_x],
                dst_ref=turned.at[i, here],
                send_sem=b_send,
                recv_sem=b_recv.at[i],
                device_id=device(z, to_x, to_y, c),
                device_id_type=MESH,
            ).start()

    def send(i, to_z, into, to_c):
        pltpu.make_async_remote_copy(
            src_ref=sent.at[i, to_c],
            dst_ref=arrived.at[into],
            send_sem=a_send,
            recv_sem=a_recv.at[into],
            device_id=device(to_z, x, y, to_c),
            device_id_type=MESH,
        ).start()

    def ship(i, to_c):
        send(i, goes_to(i), slot, to_c)

    get_had.wait()
    turn(0)
    pl.semaphore_wait(barrier, 30)
    over = pltpu.make_async_remote_copy(
        src_ref=half.at[0],
        dst_ref=half.at[WAVES],
        send_sem=p_sem.at[0],
        recv_sem=p_sem.at[1],
        device_id=device(across, x, y, c),
        device_id_type=MESH,
    )
    over.start()
    turn(1)
    spread(1, 1)
    top[...] = jnp.zeros_like(top)
    get_mix.wait()

    ids = (lax.broadcasted_iota(jnp.int32, (32, 32), 0), lax.broadcasted_iota(jnp.int32, (32, 32), 1))
    owner = jnp.broadcast_to(owner_ref[...], (32, 32)).astype(jnp.float32)
    other = column_of(owner, diagonal(32, 32))
    before = (owner < other) | ((owner == other) & (ids[1] < ids[0]))
    position = jnp.sum(before.astype(jnp.float32), axis=1, keepdims=True)
    chosen = jnp.where(position == ids[1].astype(jnp.float32), ids[0].astype(jnp.float32), 0.0)
    order_vmem[...] = jnp.sum(chosen, axis=0, keepdims=True).astype(jnp.int32)
    put_order = pltpu.make_async_copy(order_vmem, order_ref, t_sem.at[0])
    put_order.start()
    put_order.wait()

    @pl.loop(0, WAVES)
    def _(step):
        i = lax.rem(step + 1, WAVES)
        crossed = i == 0

        @pl.when(step < WAVES - 2)
        def _():
            turn(i + 1)
            spread(i + 1, i + 1)

        @pl.when(step == WAVES - 2)
        def _():
            over.wait()
            spread(WAVES, 0)

        landed = turned.at[i, pl.ds(0, GROUP - 1)]
        pltpu.make_async_copy(landed, landed, b_recv.at[i]).wait()

        cells = [
            jnp.concatenate(
                [
                    turned[i, f * 2 + e, :, t * HAD : (t + 1) * HAD]
                    for f in range(8)
                    for t in range(TILES)
                ],
                axis=0,
            )
            for e in range(2)
        ]
        res[...] = jnp.dot(
            mix_ref[...], jnp.concatenate(cells, axis=1), preferred_element_type=jnp.float32
        )
        which = jnp.where(crossed, 1, 0)
        for k in range(COS):
            for e in range(2):
                best = top[which, e, k]
                for to_c in range(2):
                    got = res[k * ROWS + to_c * 8 : k * ROWS + to_c * 8 + 8, e * HAD : (e + 1) * HAD]
                    best = jnp.maximum(best, jnp.abs(got))
                    sent[i, to_c, e, :, k * HAD : (k + 1) * HAD] = got.astype(jnp.bfloat16)
                top[which, e, k] = best

        @pl.when(step < HELD)
        def _():
            ship(i, 1)
            ship(i, 0)

        @pl.when(step >= WAVES - 2)
        def _():
            into = jnp.where(crossed, across * 2 + c, slot)
            send(i, z, into, 1 - c)
            pltpu.make_async_copy(sent.at[i, c], arrived.at[into], a_recv.at[into]).start()

    mask = diagonal(COS, HAD)
    rows = []
    for which in range(2):
        largest = jnp.max(jnp.max(top[which], axis=2), axis=2, keepdims=True)
        rows += [jnp.sum(jnp.where(mask, largest[e], 0.0), axis=0, keepdims=True) for e in range(2)]
    mine = jnp.concatenate(rows + [jnp.zeros((4, HAD), jnp.float32)], axis=0)
    lines[...] = mine
    tops[slot] = mine

    @pl.loop(1, GROUP)
    def _(o):
        pltpu.make_async_remote_copy(
            src_ref=lines,
            dst_ref=tops.at[slot],
            send_sem=s_send,
            recv_sem=s_recv,
            device_id=device(lax.rem(z + o // 2, 8), x, y, lax.rem(c + o, 2)),
            device_id_type=MESH,
        ).start()

    @pl.loop(HELD, LAST)
    def _(step):
        ship(step + 1, 1)
        ship(step + 1, 0)

    others = tops.at[pl.ds(0, GROUP - 1)]
    pltpu.make_async_copy(others, others, s_recv).wait()
    for e in range(2):
        crossing = jnp.concatenate([tops[8:, 2 + e, :], tops[:8, 2 + e, :]], axis=0)
        scales_ref[low, e] = jnp.maximum(tops[:, e, :], crossing) + jnp.float32(EPS)
    pair = pltpu.make_async_remote_copy(
        src_ref=scales_ref.at[low],
        dst_ref=scales_ref.at[low],
        send_sem=pair_sem.at[0],
        recv_sem=pair_sem.at[1],
        device_id=device(z, x + 1 - 2 * low, y, c),
        device_id_type=MESH,
    )
    pair.start()

    @pl.loop(LAST, WAVES - 2)
    def _(step):
        ship(step + 1, 1)
        ship(step + 1, 0)

    @pl.loop(0, GROUP)
    def _(s):
        for e in range(2):
            column = column_of(scales_ref[low, e, pl.ds(s, 1), :], mask)
            factors[s, e] = jnp.broadcast_to(1.0 / column, (COS, HAD))

    @pl.loop(0, GROUP)
    def _(step):
        from_z = lax.rem(z + 8 - wave_step(lax.rem(step // 2 + 7, 8)), 8)
        s = from_z * 2 + lax.rem(step, 2)
        pltpu.make_async_copy(arrived.at[s], arrived.at[s], a_recv.at[s]).wait()
        for e in range(2):
            for k in range(COS):
                cell = arrived[s, e, :, k * HAD : (k + 1) * HAD].astype(jnp.float32)
                cell = cell * factors[s, e, k : k + 1, :]
                out_ref[s, e, :, k * HAD : (k + 1) * HAD] = cell.astype(jnp.bfloat16)

    pltpu.make_async_copy(others, others, s_send).wait()
    pair.wait()
    parts = half.at[pl.ds(0, WAVES), pl.ds(0, GROUP - 1)]
    pltpu.make_async_copy(parts, parts, b_send).wait()
    shipped = arrived.at[pl.ds(0, GROUP - 2)]
    pltpu.make_async_copy(shipped, shipped, a_send).wait()


def order_kernel(order_ref, data_ref, scales_ref, out_ref, lines_ref, lines, sem, lines_sem):
    count = out_ref.shape[0]

    @pl.loop(0, count)
    def _(p):
        e = order_ref[0, p]
        pltpu.make_async_copy(data_ref.at[lax.rem(e, GROUP), e // GROUP], out_ref.at[p], sem).start()

    @pl.loop(0, count)
    def _(p):
        e = order_ref[0, p]
        for b in range(2):
            lines[p, b : b + 1, :] = scales_ref[b, e // GROUP, pl.ds(lax.rem(e, GROUP), 1), :][:, :COS]

    put = pltpu.make_async_copy(lines, lines_ref, lines_sem)
    put.start()
    pltpu.make_async_copy(out_ref, out_ref, sem).wait()
    put.wait()


def per_device(weights, owner_map):
    bf16, f32 = jnp.bfloat16, jnp.float32
    had = np.kron(np.eye(2, dtype=np.float32), hadamard()).astype(ml_dtypes.bfloat16)
    mix = np.kron(cosine(), np.eye(ROWS, dtype=np.float32)).astype(ml_dtypes.bfloat16)
    vmem = pl.BlockSpec(memory_space=pltpu.VMEM)
    smem = pl.BlockSpec(memory_space=pltpu.SMEM)
    anywhere = pl.BlockSpec(memory_space=pl.ANY)
    hbm = pl.BlockSpec(memory_space=pltpu.HBM)
    count = owner_map.shape[0]
    dma = pltpu.SemaphoreType.DMA
    moved, scales, order = pl.pallas_call(
        move_kernel,
        out_shape=(
            pltpu.VMEM((GROUP, 2, 8, D), bf16),
            pltpu.VMEM((2, 2, GROUP, HAD), f32),
            pltpu.SMEM((1, count), jnp.int32),
        ),
        in_specs=[hbm, hbm, hbm, vmem],
        out_specs=(vmem, vmem, smem),
        scratch_shapes=[
            pltpu.VMEM(had.shape, bf16),
            pltpu.VMEM(mix.shape, bf16),
            pltpu.VMEM((WAVES, GROUP, ROWS, WIDE), bf16),
            pltpu.VMEM((WAVES + 1, GROUP, ROWS, WIDE), bf16),
            pltpu.VMEM((WAVES, GROUP, ROWS, WIDE), bf16),
            pltpu.VMEM((COS * ROWS, 2 * HAD), f32),
            pltpu.VMEM((WAVES, 2, 2, 8, D), bf16),
            pltpu.VMEM((GROUP, 2, 8, D), bf16),
            pltpu.VMEM((2, 2, COS, 8, HAD), f32),
            pltpu.VMEM((8, HAD), f32),
            pltpu.VMEM((GROUP, 8, HAD), f32),
            pltpu.VMEM((GROUP, 2, COS, HAD), f32),
            pltpu.VMEM((1, count), jnp.int32),
            dma((2,)),
            dma((WAVES,)),
            dma((2,)),
            dma,
            dma((WAVES,)),
            dma,
            dma((GROUP,)),
            dma((2,)),
            dma,
            dma,
        ],
        compiler_params=pltpu.CompilerParams(
            collective_id=0, has_side_effects=True, vmem_limit_bytes=52 * 2**20
        ),
        name="move",
    )(
        weights.reshape(GROUP, WAVES, ROWS, WIDE),
        jnp.asarray(had),
        jnp.asarray(mix),
        owner_map.reshape(1, count),
    )
    quant, lines = pl.pallas_call(
        order_kernel,
        out_shape=(
            jax.ShapeDtypeStruct((count, 8, D), bf16),
            jax.ShapeDtypeStruct((count, 2, COS), f32),
        ),
        in_specs=[smem, vmem, vmem],
        out_specs=(anywhere, anywhere),
        scratch_shapes=[
            pltpu.VMEM((count, 2, COS), f32),
            dma,
            dma,
        ],
        compiler_params=pltpu.CompilerParams(vmem_limit_bytes=8 * 2**20),
        name="order",
    )(order, moved, scales)
    return quant.reshape(count, 1, 8, D), lines


def solution(mesh):
    return jax.shard_map(
        per_device,
        mesh=mesh,
        in_specs=(P(("ep", "rep"), None, "fsdp"), P()),
        out_specs=(P(None, "fsdp", ("ep", "rep"), None), P(None, "fsdp", None)),
        check_vma=False,
    )
```

```python
import math

import jax
import jax.numpy as jnp
import ml_dtypes
import numpy as np
from jax import lax
from jax.experimental import pallas as pl
from jax.experimental.pallas import tpu as pltpu
from jax.sharding import PartitionSpec as P

MESH = pl.DeviceIdType.MESH
D = 7168
HAD = 128
COS = 56
WIDE = 896
TILES = WIDE // HAD
ROWS = 16
WAVES = 8
HELD = 2
LAST = 4
GROUP = 16
EPS = 1e-06


def hadamard():
    i = np.arange(HAD)
    both = i[:, None] & i[None, :]
    ones = sum((both >> bit) & 1 for bit in range(7))
    return (1 - 2 * (ones % 2)).astype(np.float32)


def cosine():
    k = np.arange(COS, dtype=np.float64)[:, None]
    j = np.arange(COS, dtype=np.float64)[None, :]
    c = np.sqrt(2.0 / COS) * np.cos(np.pi * (2 * j + 1) * k / (2 * COS))
    c[0] *= np.sqrt(0.5)
    return c.astype(ml_dtypes.bfloat16).astype(np.float32)


def device(z, x, y, c):
    return (lax.rem(x, 2) * 8 + z, y * 2 + x // 2, c)


def place():
    ep, fsdp, core = lax.axis_index("ep"), lax.axis_index("fsdp"), lax.axis_index("rep")
    return lax.rem(ep, 8), lax.rem(fsdp, 2) * 2 + ep // 8, fsdp // 2, core


def wave_step(i):
    return 4 + (1 - 2 * lax.rem(i, 2)) * ((i + 1) // 2)


def column_of(line, mask):
    return jnp.sum(jnp.where(mask, line, 0.0), axis=1, keepdims=True)


def diagonal(rows, lanes):
    return lax.broadcasted_iota(jnp.int32, (rows, lanes), 0) == lax.broadcasted_iota(
        jnp.int32, (rows, lanes), 1
    )


def move_kernel(
    w_ref, had_hbm, mix_hbm, owner_ref, out_ref, scales_ref, order_ref,
    had_ref, mix_ref, w_buf, half, turned, res, sent, arrived, top, lines, tops, factors, order_vmem,
    t_sem, w_sem, p_sem, b_send, b_recv, a_send, a_recv, pair_sem, s_send, s_recv,
):
    z, x, y, c = place()
    here = y * 4 + x
    slot = z * 2 + c
    low = lax.rem(x, 2)
    across = lax.rem(z + 4, 8)

    def goes_to(i):
        return lax.rem(z + wave_step(i), 8)

    def fetch(i):
        return pltpu.make_async_copy(w_ref.at[:, goes_to(i)], w_buf.at[i], w_sem.at[i])

    get_had = pltpu.make_async_copy(had_hbm, had_ref, t_sem.at[0])
    get_mix = pltpu.make_async_copy(mix_hbm, mix_ref, t_sem.at[1])
    get_had.start()
    fetch(0).start()

    barrier = pltpu.get_barrier_semaphore()
    for dz in (4, 3, 5, 2, 6, 1, 7, 0):
        for dc in range(2):
            if dz or dc:
                pl.semaphore_signal(
                    barrier, inc=1, device_id_type=MESH,
                    device_id=device(lax.rem(z + dz, 8), x, y, lax.rem(c + dc, 2)),
                )
    for o in range(1, GROUP):
        pl.semaphore_signal(
            barrier, inc=1, device_id_type=MESH,
            device_id=device(z, lax.rem(x + o % 4, 4), lax.rem(y + o // 4, 4), c),
        )

    def turn(i):
        fetch(i).wait()
        rows = w_buf[i].reshape(GROUP * ROWS, WIDE)
        for first in range(0, WIDE, 256):
            wide = min(256, WIDE - first)
            got = jnp.dot(
                rows[:, first : first + wide], had_ref[:wide, :wide], preferred_element_type=jnp.float32
            ) * jnp.float32(1.0 / math.sqrt(HAD))
            half[i, :, :, first : first + wide] = got.astype(jnp.bfloat16).reshape(GROUP, ROWS, wide)

    def spread(source, i):
        turned[i, here] = half[source, here]

        @pl.loop(1, GROUP)
        def _(o):
            to_x, to_y = lax.rem(x + lax.rem(o, 4), 4), lax.rem(y + o // 4, 4)
            pltpu.make_async_remote_copy(
                src_ref=half.at[source, to_y * 4 + to_x],
                dst_ref=turned.at[i, here],
                send_sem=b_send,
                recv_sem=b_recv.at[i],
                device_id=device(z, to_x, to_y, c),
                device_id_type=MESH,
            ).start()

    def send(i, to_z, into, to_c):
        pltpu.make_async_remote_copy(
            src_ref=sent.at[i, to_c],
            dst_ref=arrived.at[into],
            send_sem=a_send,
            recv_sem=a_recv.at[into],
            device_id=device(to_z, x, y, to_c),
            device_id_type=MESH,
        ).start()

    def ship(i, to_c):
        send(i, goes_to(i), slot, to_c)

    get_had.wait()
    turn(0)
    pl.semaphore_wait(barrier, 30)
    over = pltpu.make_async_remote_copy(
        src_ref=half.at[0],
        dst_ref=half.at[WAVES],
        send_sem=p_sem.at[0],
        recv_sem=p_sem.at[1],
        device_id=device(across, x, y, c),
        device_id_type=MESH,
    )
    over.start()

    @pl.loop(1, WAVES)
    def _(i):
        fetch(i).start()

    get_mix.start()
    turn(1)
    spread(1, 1)
    top[...] = jnp.zeros_like(top)
    get_mix.wait()

    ids = (lax.broadcasted_iota(jnp.int32, (32, 32), 0), lax.broadcasted_iota(jnp.int32, (32, 32), 1))
    owner = jnp.broadcast_to(owner_ref[...], (32, 32)).astype(jnp.float32)
    other = column_of(owner, diagonal(32, 32))
    before = (owner < other) | ((owner == other) & (ids[1] < ids[0]))
    position = jnp.sum(before.astype(jnp.float32), axis=1, keepdims=True)
    chosen = jnp.where(position == ids[1].astype(jnp.float32), ids[0].astype(jnp.float32), 0.0)
    order_vmem[...] = jnp.sum(chosen, axis=0, keepdims=True).astype(jnp.int32)
    put_order = pltpu.make_async_copy(order_vmem, order_ref, t_sem.at[0])
    put_order.start()
    put_order.wait()

    @pl.loop(0, WAVES)
    def _(step):
        i = lax.rem(step + 1, WAVES)
        crossed = i == 0

        @pl.when(step < WAVES - 2)
        def _():
            turn(i + 1)
            spread(i + 1, i + 1)

        @pl.when(step == WAVES - 2)
        def _():
            over.wait()
            spread(WAVES, 0)

        landed = turned.at[i, pl.ds(0, GROUP - 1)]
        pltpu.make_async_copy(landed, landed, b_recv.at[i]).wait()

        cells = [
            jnp.concatenate(
                [
                    turned[i, f * 2 + e, :, t * HAD : (t + 1) * HAD]
                    for f in range(8)
                    for t in range(TILES)
                ],
                axis=0,
            )
            for e in range(2)
        ]
        res[...] = jnp.dot(
            mix_ref[...], jnp.concatenate(cells, axis=1), preferred_element_type=jnp.float32
        )
        which = jnp.where(crossed, 1, 0)
        for k in range(COS):
            for e in range(2):
                best = top[which, e, k]
                for to_c in range(2):
                    got = res[k * ROWS + to_c * 8 : k * ROWS + to_c * 8 + 8, e * HAD : (e + 1) * HAD]
                    best = jnp.maximum(best, jnp.abs(got))
                    sent[i, to_c, e, :, k * HAD : (k + 1) * HAD] = got.astype(jnp.bfloat16)
                top[which, e, k] = best

        @pl.when(step < HELD)
        def _():
            ship(i, 1)
            ship(i, 0)

        @pl.when(step >= WAVES - 2)
        def _():
            into = jnp.where(crossed, across * 2 + c, slot)
            send(i, z, into, 1 - c)
            pltpu.make_async_copy(sent.at[i, c], arrived.at[into], a_recv.at[into]).start()

    mask = diagonal(COS, HAD)
    rows = []
    for which in range(2):
        largest = jnp.max(jnp.max(top[which], axis=2), axis=2, keepdims=True)
        rows += [jnp.sum(jnp.where(mask, largest[e], 0.0), axis=0, keepdims=True) for e in range(2)]
    mine = jnp.concatenate(rows + [jnp.zeros((4, HAD), jnp.float32)], axis=0)
    lines[...] = mine
    tops[slot] = mine

    @pl.loop(1, GROUP)
    def _(o):
        pltpu.make_async_remote_copy(
            src_ref=lines,
            dst_ref=tops.at[slot],
            send_sem=s_send,
            recv_sem=s_recv,
            device_id=device(lax.rem(z + o // 2, 8), x, y, lax.rem(c + o, 2)),
            device_id_type=MESH,
        ).start()

    @pl.loop(HELD, LAST)
    def _(step):
        ship(step + 1, 1)
        ship(step + 1, 0)

    others = tops.at[pl.ds(0, GROUP - 1)]
    pltpu.make_async_copy(others, others, s_recv).wait()
    for e in range(2):
        crossing = jnp.concatenate([tops[8:, 2 + e, :], tops[:8, 2 + e, :]], axis=0)
        scales_ref[low, e] = jnp.maximum(tops[:, e, :], crossing) + jnp.float32(EPS)
    pair = pltpu.make_async_remote_copy(
        src_ref=scales_ref.at[low],
        dst_ref=scales_ref.at[low],
        send_sem=pair_sem.at[0],
        recv_sem=pair_sem.at[1],
        device_id=device(z, x + 1 - 2 * low, y, c),
        device_id_type=MESH,
    )
    pair.start()

    @pl.loop(LAST, WAVES - 2)
    def _(step):
        ship(step + 1, 1)
        ship(step + 1, 0)

    @pl.loop(0, GROUP)
    def _(s):
        for e in range(2):
            column = column_of(scales_ref[low, e, pl.ds(s, 1), :], mask)
            factors[s, e] = jnp.broadcast_to(1.0 / column, (COS, HAD))

    @pl.loop(0, GROUP)
    def _(step):
        from_z = lax.rem(z + 8 - wave_step(lax.rem(step // 2 + 7, 8)), 8)
        s = from_z * 2 + lax.rem(step, 2)
        pltpu.make_async_copy(arrived.at[s], arrived.at[s], a_recv.at[s]).wait()
        for e in range(2):
            for k in range(COS):
                cell = arrived[s, e, :, k * HAD : (k + 1) * HAD].astype(jnp.float32)
                cell = cell * factors[s, e, k : k + 1, :]
                out_ref[s, e, :, k * HAD : (k + 1) * HAD] = cell.astype(jnp.bfloat16)

    pltpu.make_async_copy(others, others, s_send).wait()
    pair.wait()
    parts = half.at[pl.ds(0, WAVES), pl.ds(0, GROUP - 1)]
    pltpu.make_async_copy(parts, parts, b_send).wait()
    shipped = arrived.at[pl.ds(0, GROUP - 2)]
    pltpu.make_async_copy(shipped, shipped, a_send).wait()


def order_kernel(order_ref, data_ref, scales_ref, out_ref, lines_ref, lines, sem, lines_sem):
    count = out_ref.shape[0]

    @pl.loop(0, count)
    def _(p):
        e = order_ref[0, p]
        pltpu.make_async_copy(data_ref.at[lax.rem(e, GROUP), e // GROUP], out_ref.at[p], sem).start()

    @pl.loop(0, count)
    def _(p):
        e = order_ref[0, p]
        for b in range(2):
            lines[p, b : b + 1, :] = scales_ref[b, e // GROUP, pl.ds(lax.rem(e, GROUP), 1), :][:, :COS]

    put = pltpu.make_async_copy(lines, lines_ref, lines_sem)
    put.start()
    pltpu.make_async_copy(out_ref, out_ref, sem).wait()
    put.wait()


def per_device(weights, owner_map):
    bf16, f32 = jnp.bfloat16, jnp.float32
    had = np.kron(np.eye(2, dtype=np.float32), hadamard()).astype(ml_dtypes.bfloat16)
    mix = np.kron(cosine(), np.eye(ROWS, dtype=np.float32)).astype(ml_dtypes.bfloat16)
    vmem = pl.BlockSpec(memory_space=pltpu.VMEM)
    smem = pl.BlockSpec(memory_space=pltpu.SMEM)
    anywhere = pl.BlockSpec(memory_space=pl.ANY)
    hbm = pl.BlockSpec(memory_space=pltpu.HBM)
    count = owner_map.shape[0]
    dma = pltpu.SemaphoreType.DMA
    moved, scales, order = pl.pallas_call(
        move_kernel,
        out_shape=(
            pltpu.VMEM((GROUP, 2, 8, D), bf16),
            pltpu.VMEM((2, 2, GROUP, HAD), f32),
            pltpu.SMEM((1, count), jnp.int32),
        ),
        in_specs=[hbm, hbm, hbm, vmem],
        out_specs=(vmem, vmem, smem),
        scratch_shapes=[
            pltpu.VMEM(had.shape, bf16),
            pltpu.VMEM(mix.shape, bf16),
            pltpu.VMEM((WAVES, GROUP, ROWS, WIDE), bf16),
            pltpu.VMEM((WAVES + 1, GROUP, ROWS, WIDE), bf16),
            pltpu.VMEM((WAVES, GROUP, ROWS, WIDE), bf16),
            pltpu.VMEM((COS * ROWS, 2 * HAD), f32),
            pltpu.VMEM((WAVES, 2, 2, 8, D), bf16),
            pltpu.VMEM((GROUP, 2, 8, D), bf16),
            pltpu.VMEM((2, 2, COS, 8, HAD), f32),
            pltpu.VMEM((8, HAD), f32),
            pltpu.VMEM((GROUP, 8, HAD), f32),
            pltpu.VMEM((GROUP, 2, COS, HAD), f32),
            pltpu.VMEM((1, count), jnp.int32),
            dma((2,)),
            dma((WAVES,)),
            dma((2,)),
            dma,
            dma((WAVES,)),
            dma,
            dma((GROUP,)),
            dma((2,)),
            dma,
            dma,
        ],
        compiler_params=pltpu.CompilerParams(
            collective_id=0, has_side_effects=True, vmem_limit_bytes=52 * 2**20
        ),
        name="move",
    )(
        weights.reshape(GROUP, WAVES, ROWS, WIDE),
        jnp.asarray(had),
        jnp.asarray(mix),
        owner_map.reshape(1, count),
    )
    quant, lines = pl.pallas_call(
        order_kernel,
        out_shape=(
            jax.ShapeDtypeStruct((count, 8, D), bf16),
            jax.ShapeDtypeStruct((count, 2, COS), f32),
        ),
        in_specs=[smem, vmem, vmem],
        out_specs=(anywhere, anywhere),
        scratch_shapes=[
            pltpu.VMEM((count, 2, COS), f32),
            dma,
            dma,
        ],
        compiler_params=pltpu.CompilerParams(vmem_limit_bytes=8 * 2**20),
        name="order",
    )(order, moved, scales)
    return quant.reshape(count, 1, 8, D), lines


def solution(mesh):
    return jax.shard_map(
        per_device,
        mesh=mesh,
        in_specs=(P(("ep", "rep"), None, "fsdp"), P()),
        out_specs=(P(None, "fsdp", ("ep", "rep"), None), P(None, "fsdp", None)),
        check_vma=False,
    )
```
